256 devices in a mesh: tm: 64 (over y, x, z_lo), lat: 4 (over z_hi, core).
Axes of the slice: x: 4, y: 4, z: 8 (z_hi: 2, z_lo: 4; z = z_hi * 4 + z_lo), core: 2. Of those that a mesh axis runs over, the one named last changes fastest.
Arguments:
- incr_static: float32 [64, 32, 192, 128], P('tm', 'lat'), may hold values from -6 to 6
- ens_pert: bfloat16 [8, 64, 32, 192, 128], P(None, 'tm', 'lat'), may hold values from -0.59765625 to 0.59765625
- ens_weight: float32 [8, 4, 1024], P(None, 'lat', 'tm'), may hold values from -6 to 6
- column_map: int32 [32, 192], P('lat'), may hold values from 0 to 1023
- sub_steps: int32 [64], P('tm'), may hold values from 1 to 4, 192 in all
- diffusion: bfloat16 [64, 32, 192, 128], P('tm', 'lat'), may hold values from 0.0099487305 to 0.23925781
- mode_in: bfloat16 [4, 128, 128], replicated, may hold values from -0.5 to 0.5
- mode_out: bfloat16 [4, 128, 128], replicated, may hold values from -0.25 to 0.25
- model_precision: bfloat16 [64, 32, 192, 128], P('tm', 'lat'), may hold values from 0.099609375 to 1
- obs_precision: bfloat16 [64, 32, 192, 128], P('tm', 'lat'), may hold values from 0.099609375 to 1
- innovation: bfloat16 [64, 32, 192, 128], P('tm', 'lat'), may hold values from -6 to 6
Outputs:
- grad_static: float32 [64, 32, 192, 128], P('tm', 'lat')
- grad_weight: float32 [8, 4, 1024], P(None, 'lat', 'tm')
The draws below stay inside these ranges and needn't reach their ends.
Inputs may be any that keep to these rules, and one draw needn't show every extreme that they name: `column_map`: each cell names one of the 1024 weight columns of its own latitude slab. `sub_steps`: the subwindows' step counts add up to 192.
All inputs are finite; a program needn't handle non-finite values. No bound on the sum of `sub_steps` on one device may be relied on, other than what follows from the above.
Results may differ from the reference program's by a relative error of at most 0.0065.
Values may be sent and summed in bfloat16 or wider, within the bound.
No kernel may reach another device: no remote copies, remote signals or barrier semaphores. Data moves between devices by JAX's collectives and lax.ppermute only.
A program may use at most 64 MiB of HBM per device.

```python
import math
import jax
import jax.numpy as jnp
import numpy as np
from jax import lax

LAT_DEV = 8
LON = 192
LEV = 128
MEM = 8
STEPS = 4
SUB = 64
LATS = 32
SLABS = 4
CSLAB = 1024


def place_ends(entries, rng, low, high):
    index_at = [jax.random.randint(jax.random.fold_in(rng, axis), (), 0, length) for axis, length in enumerate(entries.shape)]
    main_axis = entries.shape.index(max(entries.shape))
    neighbour = index_at[:main_axis] + [(index_at[main_axis] + 1) % entries.shape[main_axis]] + index_at[main_axis + 1:]
    return entries.at[tuple(index_at)].set(low).at[tuple(neighbour)].set(high)


def block_scale(rng, dims, pieces, low, largest):
    level, own = 1.0, jax.random.fold_in(rng, 6)
    for axis_at, shards_of in pieces:
        draws = jnp.exp(jax.random.uniform(jax.random.fold_in(own, axis_at), (shards_of,), jnp.float32, low / len(pieces), largest / len(pieces)))
        level = level * jnp.repeat(draws, dims[axis_at] // shards_of).reshape([-1 if axis == axis_at else 1 for axis in range(len(dims))])
    return level


def profile(count, total, limit, skew):
    weights = [(1 << 20) // math.isqrt(standing ** skew) + 1 for standing in range(2, count + 1)]
    surplus, holding = total - limit - (count - 1), [1] * (count - 1)
    while surplus > 0:
        free = [i for i in range(count - 1) if holding[i] < limit]
        whole, left = sum([weights[i] for i in free]), surplus
        for i in free:
            addition = min(limit - holding[i], max(1, left * weights[i] // whole), surplus)
            holding[i] = holding[i] + addition
            surplus = surplus - addition
    return np.array([limit] + holding)


def uneven_parts(rng, count, total, limit, slope):
    if count == 2:
        one = jax.random.randint(rng, (), max(1, total - limit), min(limit, total - 1) + 1)
        return jnp.stack([one, total - one])
    sizes = jnp.asarray(profile(count, total, limit, slope), jnp.int32)
    couples = (count - 1) // 2
    donor, sink = sizes[1:1 + 2 * couples:2], sizes[2:2 + 2 * couples:2]
    margin = jnp.minimum(donor - 1, limit - sink)
    passed = jax.random.randint(jax.random.fold_in(rng, 1), (couples,), 0, 1 << 20) % (margin + 1)
    sizes = sizes.at[1:1 + 2 * couples:2].set(donor - passed).at[2:2 + 2 * couples:2].set(sink + passed)
    return sizes[jax.random.permutation(jax.random.fold_in(rng, 2), count)]


def noise(stream_key, extent, scale, bound, shards=(), held_as=jnp.bfloat16):
    values = jax.random.normal(stream_key, extent, jnp.float32) * scale
    if len(shards) > 0:
        values = block_scale(stream_key, extent, shards, -0.22, 0.18) * values
    return jnp.clip(values, min=-bound, max=bound).astype(held_as)


def setup_inputs(seed: int = 0) -> dict:
    streams_of = jax.random.split(jax.random.key(seed), 12)
    incr_static = noise(streams_of[0], (SUB, LATS, LON, LEV), 1.0, 6.0, ((0, 64), (1, 4)), jnp.float32)
    ens_pert = noise(streams_of[1], (MEM, SUB, LATS, LON, LEV), 0.1, 0.59765625, ((1, 64), (2, 4)))
    ens_weight = noise(streams_of[2], (MEM, SLABS, CSLAB), 1.0, 6.0, ((1, 4), (2, 64)), jnp.float32)
    column_map = place_ends(jax.random.randint(streams_of[3], (LATS, LON), 0, CSLAB), jax.random.fold_in(streams_of[3], 1), 0, CSLAB - 1).astype(jnp.int32)
    sub_steps = uneven_parts(streams_of[4], SUB, 3 * SUB, STEPS, 0).astype(jnp.int32)
    diffusion = jnp.clip(jnp.exp(math.log(0.23925781) - 3.1800967 * jax.random.uniform(streams_of[5], (SUB, LATS, LON, LEV), jnp.float32) ** block_scale(streams_of[5], (SUB, LATS, LON, LEV), ((0, 64), (1, 4)), -0.2, 0.2)), 0.0099487305, 0.23925781).astype(jnp.bfloat16)
    mode_in = noise(streams_of[6], (STEPS, LEV, LEV), LEV ** -0.5, 0.5)
    mode_out = noise(streams_of[7], (STEPS, LEV, LEV), (4 * LEV) ** -0.5, 0.25)
    model_precision = jnp.clip(jnp.exp(math.log(1.0) - 2.306499 * jax.random.uniform(streams_of[8], (SUB, LATS, LON, LEV), jnp.float32) ** block_scale(streams_of[8], (SUB, LATS, LON, LEV), ((0, 64), (1, 4)), -0.2, 0.2)), 0.099609375, 1.0).astype(jnp.bfloat16)
    obs_precision = jnp.clip(jnp.exp(math.log(1.0) - 2.306499 * jax.random.uniform(streams_of[9], (SUB, LATS, LON, LEV), jnp.float32) ** block_scale(streams_of[9], (SUB, LATS, LON, LEV), ((0, 64), (1, 4)), -0.2, 0.2)), 0.099609375, 1.0).astype(jnp.bfloat16)
    innovation = noise(streams_of[10], (SUB, LATS, LON, LEV), 1.0, 6.0, ((0, 64), (1, 4)))
    return {"incr_static": incr_static, "ens_pert": ens_pert, "ens_weight": ens_weight, "column_map": column_map, "sub_steps": sub_steps, "diffusion": diffusion, "mode_in": mode_in, "mode_out": mode_out, "model_precision": model_precision, "obs_precision": obs_precision, "innovation": innovation}


def laplace(state_field):
    padded = jnp.pad(state_field, ((1, 1), (0, 0), (0, 0)))
    return (padded[2:] + padded[:-2] + jnp.roll(state_field, 1, axis=1)
            + jnp.roll(state_field, -1, axis=1) - 4.0 * state_field)


def vertical(smoothed, to_modes, from_modes):
    layout = smoothed.shape
    flat = smoothed.astype(jnp.bfloat16).reshape(-1, layout[-1])
    mode_values = jnp.dot(flat, to_modes, preferred_element_type=jnp.float32).astype(jnp.bfloat16)
    return jnp.dot(mode_values, from_modes, preferred_element_type=jnp.float32).reshape(layout)


def tangent(state_field, diffuse, step_count, mode_in, mode_out):
    for section in range(STEPS):
        smoothed = state_field + diffuse * laplace(state_field)
        advanced = smoothed + vertical(smoothed, mode_in[section], mode_out[section])
        state_field = jnp.where(section < step_count, advanced, state_field)
    return state_field


def adjoint(state_field, diffuse, step_count, mode_in, mode_out):
    for section in reversed(range(STEPS)):
        coupled = state_field + vertical(state_field, mode_out[section].T, mode_in[section].T)
        advanced = coupled + laplace(diffuse * coupled)
        state_field = jnp.where(section < step_count, advanced, state_field)
    return state_field


def reference(incr_static, ens_pert, ens_weight, column_map, sub_steps, diffusion, mode_in, mode_out,
              model_precision, obs_precision, innovation):
    row_slab = (jnp.arange(LATS, dtype=jnp.int32) // LAT_DEV).astype(jnp.int32)
    member_weight = jnp.take_along_axis(ens_weight[:, row_slab, :], column_map[None], axis=2)
    segment_ids = (row_slab[:, None] * CSLAB + column_map).reshape(-1)

    def start_of(window):
        pert_here = lax.dynamic_index_in_dim(ens_pert, window, 1, keepdims=False)
        return incr_static[window] + jnp.sum(pert_here.astype(jnp.float32) * member_weight[..., None], axis=0)

    def run(window):
        return tangent(start_of(window), diffusion[window].astype(jnp.float32), sub_steps[window], mode_in, mode_out)

    windows = jnp.arange(SUB, dtype=jnp.int32)
    end_state = lax.map(run, windows)

    def jump_of(window):
        earlier = lax.dynamic_index_in_dim(end_state, jnp.maximum(window - 1, 0), 0, keepdims=False)
        earlier = jnp.where(window > 0, earlier, jnp.zeros_like(earlier))
        return model_precision[window].astype(jnp.float32) * (start_of(window) - earlier)

    def gradient_of(window):
        own_jump = jump_of(window)
        next_jump = jump_of(jnp.minimum(window + 1, SUB - 1))
        next_jump = jnp.where(window + 1 < SUB, next_jump, jnp.zeros_like(next_jump))
        misfit = obs_precision[window].astype(jnp.float32) * (end_state[window] - innovation[window].astype(jnp.float32))
        gradient = own_jump + adjoint(misfit - next_jump, diffusion[window].astype(jnp.float32),
                                      sub_steps[window], mode_in, mode_out)
        pert_here = lax.dynamic_index_in_dim(ens_pert, window, 1, keepdims=False)
        contrib = jnp.sum(pert_here.astype(jnp.float32) * gradient[None], axis=-1)
        summed = jax.ops.segment_sum(contrib.reshape(MEM, -1).T, segment_ids, num_segments=SLABS * CSLAB)
        return gradient, summed.T.reshape(MEM, SLABS, CSLAB)

    gradients, partial_terms = lax.map(gradient_of, windows)
    return gradients, ens_weight + jnp.sum(partial_terms, axis=0)
```

```python
import jax
import jax.numpy as jnp
from jax import lax
from jax.experimental import pallas as pl
from jax.experimental.pallas import tpu as pltpu
from jax.sharding import PartitionSpec as P

STEPS = 4
HALO = STEPS
F32 = jnp.float32
BF16 = jnp.bfloat16
VMEM_LIMIT = 40 * 1024 * 1024

VM = pl.BlockSpec(memory_space=pltpu.VMEM)
SM = pl.BlockSpec(memory_space=pltpu.SMEM)


def iota(shape, dim):
    return lax.broadcasted_iota(jnp.int32, shape, dim)


def call(kernel, outs, scratch, specs, flops, nbytes):
    return pl.pallas_call(
        kernel,
        out_shape=outs,
        in_specs=specs,
        out_specs=jax.tree.map(lambda _: VM, outs),
        scratch_shapes=scratch,
        compiler_params=pltpu.CompilerParams(vmem_limit_bytes=VMEM_LIMIT),
        cost_estimate=pl.CostEstimate(flops=flops, bytes_accessed=nbytes, transcendentals=0),
    )


def split2(values):
    high = values.astype(BF16)
    low = (values - high.astype(F32)).astype(BF16)
    return high, low


def one_hot_rows(columns, count):
    return jnp.where(iota((count, columns.shape[1]), 0) == columns, 1.0, 0.0).astype(BF16)


def lane_selector(per):
    return jnp.where(iota((per, 128), 1) % per == iota((per, 128), 0), 1.0, 0.0).astype(BF16)


def group_spread(member, per):
    return jnp.where(iota((128, 128), 0) // per == member, 1.0, 0.0).astype(BF16)


def start_kernel(table, columns, incr, pert, start, start_half, top, bottom):
    rows, lon, lev = incr.shape
    members = pert.shape[0]
    blocks = table.shape[0]
    per = 128 // members
    held = table[...]
    high = held.astype(BF16)
    rest = held - high.astype(F32)
    middle = rest.astype(BF16)
    low = (rest - middle.astype(F32)).astype(BF16)
    empty = jnp.zeros((blocks, 128), BF16)
    right = jnp.concatenate(
        [
            jnp.concatenate([high, empty], axis=1),
            jnp.concatenate([middle, empty], axis=1),
            jnp.concatenate([low, empty], axis=1),
            jnp.concatenate([jnp.zeros((per, 128), BF16), lane_selector(per)], axis=1),
        ],
        axis=0,
    )
    for i in range(rows):
        column = columns[i : i + 1, :]
        block = one_hot_rows(column // per, blocks)
        rest_of = one_hot_rows(column % per, per)
        left = jnp.concatenate([block, block, block, rest_of], axis=0)
        both = lax.dot_general(left, right, (((0,), (0,)), ((), ())), preferred_element_type=F32)
        chosen = both[:, :128] * both[:, 128:]
        pair = jnp.concatenate(split2(chosen), axis=1)
        total = incr[i]
        for k in range(members):
            spread = group_spread(k, per)
            weight = jnp.dot(pair, jnp.concatenate([spread, spread], axis=0), preferred_element_type=F32)
            total = total + pert[k, i].astype(F32) * weight
        start[i] = total
        rounded = total.astype(BF16)
        start_half[i] = rounded
        if i < HALO:
            top[i] = rounded
        if i >= rows - HALO:
            bottom[i - (rows - HALO)] = rounded


def neighbours(field, i):
    middle = field[i]
    return (
        field[i - 1]
        + field[i + 1]
        + pltpu.roll(middle, 1, 0)
        + pltpu.roll(middle, middle.shape[0] - 1, 0)
        - 4.0 * middle
    )


def forward_kernel(
    steps, start, above, below, diffuse, diffuse_above, diffuse_below, mode_in, mode_out,
    obs, innovation, next_precision, next_start, end_half, seed, top, bottom,
    field, smooth, spread,
):
    rows, lon, lev = start.shape
    whole = rows + 2 * HALO
    for i in range(HALO):
        field[i] = above[i].astype(F32)
        field[HALO + rows + i] = below[i].astype(F32)
        spread[i] = diffuse_above[i]
        spread[HALO + rows + i] = diffuse_below[i]
    for i in range(rows):
        field[HALO + i] = start[i]
        spread[HALO + i] = diffuse[i]
    count = steps[0]
    for n in range(STEPS):

        @pl.when(n < count)
        def _():
            both = jnp.dot(mode_in[n], mode_out[n], preferred_element_type=F32).astype(BF16)
            for i in range(n + 1, whole - n - 1):
                smooth[i] = field[i] + spread[i].astype(F32) * neighbours(field, i)
            for i in range(n + 1, whole - n - 1):
                held = smooth[i]
                field[i] = held + jnp.dot(held.astype(BF16), both, preferred_element_type=F32)

    for i in range(rows):
        end = field[HALO + i]
        end_half[i] = end.astype(BF16)
        misfit = obs[i].astype(F32) * (end - innovation[i].astype(F32))
        following = next_precision[i].astype(F32) * (next_start[i].astype(F32) - end)
        value = misfit - following
        seed[i] = value
        rounded = value.astype(BF16)
        if i < HALO:
            top[i] = rounded
        if i >= rows - HALO:
            bottom[i - (rows - HALO)] = rounded


def adjoint_kernel(
    steps, seed, above, below, diffuse, diffuse_above, diffuse_below, mode_in, mode_out,
    precision, start, earlier, pert, columns, gradient, partial,
    field, scaled, spread,
):
    rows, lon, lev = seed.shape
    members = pert.shape[0]
    per = 128 // members
    blocks = partial.shape[0]
    whole = rows + 2 * HALO
    for i in range(HALO):
        field[i] = above[i].astype(F32)
        field[HALO + rows + i] = below[i].astype(F32)
        spread[i] = diffuse_above[i]
        spread[HALO + rows + i] = diffuse_below[i]
    for i in range(rows):
        field[HALO + i] = seed[i]
        spread[HALO + i] = diffuse[i]
    count = steps[0]
    for n in reversed(range(STEPS)):

        @pl.when(n < count)
        def _():
            edge = STEPS - 1 - n
            both = jnp.dot(mode_in[n], mode_out[n], preferred_element_type=F32).astype(BF16)
            for i in range(edge, whole - edge):
                held = field[i]
                coupled = held + lax.dot_general(
                    held.astype(BF16), both, (((1,), (1,)), ((), ())), preferred_element_type=F32
                )
                field[i] = coupled
                scaled[i] = spread[i].astype(F32) * coupled
            for i in range(edge + 1, whole - edge - 1):
                field[i] = field[i] + neighbours(scaled, i)

    selector = lane_selector(per)
    lane_group = iota((lon, 128), 1) // per
    total = jnp.zeros((blocks, 256), F32)
    for i in range(rows):
        jump = precision[i].astype(F32) * (start[i] - earlier[i].astype(F32))
        value = jump + field[HALO + i]
        gradient[i] = value
        terms = jnp.zeros((lon, 128), F32)
        for k in range(members):
            term = jnp.sum(pert[k, i].astype(F32) * value, axis=1, keepdims=True)
            terms = jnp.where(lane_group == k, term, terms)
        column = columns[i : i + 1, :]
        block = one_hot_rows(column // per, blocks)
        rest_of = one_hot_rows(column % per, per)
        chosen = lax.dot_general(rest_of, selector, (((0,), (0,)), ((), ())), preferred_element_type=F32)
        pair = jnp.concatenate(split2(terms * chosen), axis=1)
        total = total + jnp.dot(block, pair, preferred_element_type=F32)
    partial[...] = total[:, :128] + total[:, 128:]


def shifted(block, axis, distance):
    devices = range(lax.axis_size(axis))
    route = [(i - distance, i) for i in devices if i - distance in devices]
    return lax.ppermute(block, axis, route)


def body(
    incr_static,
    ens_pert,
    ens_weight,
    column_map,
    sub_steps,
    diffusion,
    mode_in,
    mode_out,
    model_precision,
    obs_precision,
    innovation,
):
    shape = incr_static.shape[1:]
    rows, lon, lev = shape
    members, _, per = ens_weight.shape
    windows = lax.axis_size("tm")
    half = jax.ShapeDtypeStruct(shape, BF16)
    edge = jax.ShapeDtypeStruct((HALO, lon, lev), BF16)
    full = jax.ShapeDtypeStruct(shape, F32)
    whole = (rows + 2 * HALO, lon, lev)
    pert = ens_pert[:, 0]
    diffuse = diffusion[0]
    cells = rows * lon * lev

    own = ens_weight.reshape(1, members * per)
    diffuse_above = shifted(diffuse[rows - HALO :], "lat", 1)
    diffuse_below = shifted(diffuse[:HALO], "lat", -1)
    next_precision = shifted(model_precision[0], "tm", -1)
    table = lax.all_to_all(
        jnp.broadcast_to(own, (windows, members * per)), "tm", 0, 0, tiled=True
    )
    start, start_half, top, bottom = call(
        start_kernel, (full, half, edge, edge), [], [VM] * 4, 1 << 30, 30 * cells
    )(table, column_map, incr_static[0], pert)
    above = shifted(bottom, "lat", 1)
    below = shifted(top, "lat", -1)
    next_start = shifted(start_half, "tm", -1)
    end_half, seed, top, bottom = call(
        forward_kernel,
        (half, full, edge, edge),
        [pltpu.VMEM(whole, F32), pltpu.VMEM(whole, F32), pltpu.VMEM(whole, BF16)],
        [SM] + [VM] * 12,
        1 << 30,
        30 * cells,
    )(
        sub_steps, start, above, below, diffuse, diffuse_above, diffuse_below, mode_in, mode_out,
        obs_precision[0], innovation[0], next_precision, next_start,
    )
    above = shifted(bottom, "lat", 1)
    below = shifted(top, "lat", -1)
    earlier = shifted(end_half, "tm", 1)
    gradient, partial = call(
        adjoint_kernel,
        (full, jax.ShapeDtypeStruct((windows, members * per), F32)),
        [pltpu.VMEM(whole, F32), pltpu.VMEM(whole, F32), pltpu.VMEM(whole, BF16)],
        [SM] + [VM] * 13,
        1 << 30,
        30 * cells,
    )(
        sub_steps, seed, above, below, diffuse, diffuse_above, diffuse_below, mode_in, mode_out,
        model_precision[0], start, earlier, pert, column_map,
    )
    terms = lax.all_to_all(partial, "tm", 0, 0, tiled=True)
    owned = jnp.sum(terms, axis=0).reshape(members, 1, per)
    return (gradient[None], ens_weight + owned)


def solution(mesh):
    return jax.shard_map(
        body,
        mesh=mesh,
        in_specs=(
            P("tm", "lat", None, None),
            P(None, "tm", "lat", None, None),
            P(None, "lat", "tm"),
            P("lat", None),
            P("tm"),
            P("tm", "lat", None, None),
            P(),
            P(),
            P("tm", "lat", None, None),
            P("tm", "lat", None, None),
            P("tm", "lat", None, None),
        ),
        out_specs=(P("tm", "lat", None, None), P(None, "lat", "tm")),
        check_vma=False,
    )
```

```python
import jax
import jax.numpy as jnp
from jax import lax
from jax.experimental import pallas as pl
from jax.experimental.pallas import tpu as pltpu
from jax.sharding import PartitionSpec as P

STEPS = 4
HALO = STEPS
F32 = jnp.float32
BF16 = jnp.bfloat16
VMEM_LIMIT = 40 * 1024 * 1024
COST = 1 << 20
PACK_COST = 1 << 33
START_COST = 1 << 20
FORWARD_COST = 1 << 34
ADJOINT_COST = 1 << 20

VM = pl.BlockSpec(memory_space=pltpu.VMEM)
SM = pl.BlockSpec(memory_space=pltpu.SMEM)
HB = pl.BlockSpec(memory_space=pltpu.HBM)


def iota(shape, dim):
    return lax.broadcasted_iota(jnp.int32, shape, dim)


def call(kernel, outs, scratch, specs, flops, nbytes):
    return pl.pallas_call(
        kernel,
        out_shape=outs,
        in_specs=specs,
        out_specs=jax.tree.map(lambda _: VM, outs),
        scratch_shapes=scratch,
        compiler_params=pltpu.CompilerParams(vmem_limit_bytes=VMEM_LIMIT),
        cost_estimate=pl.CostEstimate(flops=flops, bytes_accessed=nbytes, transcendentals=0),
    )


def split2(values):
    high = values.astype(BF16)
    low = (values - high.astype(F32)).astype(BF16)
    return high, low


def one_hot_rows(columns, count):
    return jnp.where(iota((count, columns.shape[1]), 0) == columns, 1.0, 0.0).astype(BF16)


def lane_selector(per):
    return jnp.where(iota((per, 128), 1) % per == iota((per, 128), 0), 1.0, 0.0).astype(BF16)


def group_spread(member, per):
    return jnp.where(iota((128, 128), 0) // per == member, 1.0, 0.0).astype(BF16)


def sides(rows):
    odd = lax.axis_index("lat") % 2
    return (1 - odd) * (rows - HALO), odd * (rows - HALO)


def pack_kernel(weight, diffuse, table, inner, outer, sems):
    rows = diffuse.shape[0]
    members, _, per = weight.shape
    near, far = sides(rows)
    copies = [
        pltpu.make_async_copy(diffuse.at[pl.ds(far, HALO)], outer, sems.at[0]),
        pltpu.make_async_copy(diffuse.at[pl.ds(near, HALO)], inner, sems.at[1]),
    ]
    for copy in copies:
        copy.start()
    held = weight[:, 0, :]
    selector = lane_selector(per)
    high = held.astype(BF16)
    rest = held - high.astype(F32)
    middle = rest.astype(BF16)
    low = (rest - middle.astype(F32)).astype(BF16)
    tiled = (
        jnp.dot(high, selector, preferred_element_type=F32)
        + jnp.dot(middle, selector, preferred_element_type=F32)
        + jnp.dot(low, selector, preferred_element_type=F32)
    )
    own = jnp.where(iota((members, 128), 1) // per == iota((members, 128), 0), tiled, 0.0)
    table[...] = jnp.broadcast_to(jnp.sum(own, axis=0, keepdims=True), table.shape)
    for copy in copies:
        copy.wait()


def take_sides(block, inner, outer):
    near, far = sides(block.shape[0])
    for i in range(HALO):
        inner[i] = block[near + i]
        outer[i] = block[far + i]


def start_kernel(table, columns, incr, pert, start, start_half, inner, outer):
    rows, lon, lev = incr.shape
    members = pert.shape[0]
    blocks = table.shape[0]
    per = 128 // members
    held = table[...]
    high = held.astype(BF16)
    rest = held - high.astype(F32)
    middle = rest.astype(BF16)
    low = (rest - middle.astype(F32)).astype(BF16)
    empty = jnp.zeros((blocks, 128), BF16)
    right = jnp.concatenate(
        [
            jnp.concatenate([high, empty], axis=1),
            jnp.concatenate([middle, empty], axis=1),
            jnp.concatenate([low, empty], axis=1),
            jnp.concatenate([jnp.zeros((per, 128), BF16), lane_selector(per)], axis=1),
        ],
        axis=0,
    )
    for i in range(rows):
        column = columns[i : i + 1, :]
        block = one_hot_rows(column // per, blocks)
        rest_of = one_hot_rows(column % per, per)
        left = jnp.concatenate([block, block, block, rest_of], axis=0)
        both = lax.dot_general(left, right, (((0,), (0,)), ((), ())), preferred_element_type=F32)
        chosen = both[:, :128] * both[:, 128:]
        pair = jnp.concatenate(split2(chosen), axis=1)
        total = incr[i]
        for k in range(members):
            spread = group_spread(k, per)
            weight = jnp.dot(pair, jnp.concatenate([spread, spread], axis=0), preferred_element_type=F32)
            total = total + pert[k, i].astype(F32) * weight
        start[i] = total
        start_half[i] = total.astype(BF16)
    take_sides(start_half, inner, outer)


def neighbours(field, i):
    middle = field[i]
    return (
        field[i - 1]
        + field[i + 1]
        + pltpu.roll(middle, 1, 0)
        + pltpu.roll(middle, middle.shape[0] - 1, 0)
        - 4.0 * middle
    )


def fill(field, spread, own, diffuse, mate, across, diffuse_mate, diffuse_across):
    rows = own.shape[0]
    odd = lax.axis_index("lat") % 2
    mate_at = (1 - odd) * (HALO + rows)
    across_at = odd * (HALO + rows)
    for i in range(HALO):
        field[mate_at + i] = mate[i].astype(F32)
        spread[mate_at + i] = diffuse_mate[i]
        field[across_at + i] = across[i].astype(F32)
        spread[across_at + i] = diffuse_across[i]
    for i in range(rows):
        field[HALO + i] = own[i]
        spread[HALO + i] = diffuse[i]


def forward_kernel(
    steps, start, across, mate, diffuse, diffuse_mate, diffuse_across, mode_in, mode_out,
    end, end_half,
    field, smooth, spread,
):
    rows, lon, lev = start.shape
    whole = rows + 2 * HALO
    fill(field, spread, start, diffuse, mate, across, diffuse_mate, diffuse_across)
    count = steps[0]
    for n in range(STEPS):

        @pl.when(n < count)
        def _():
            both = jnp.dot(mode_in[n], mode_out[n], preferred_element_type=F32).astype(BF16)
            for i in range(n + 1, whole - n - 1):
                smooth[i] = field[i] + spread[i].astype(F32) * neighbours(field, i)
            for i in range(n + 1, whole - n - 1):
                held = smooth[i]
                field[i] = held + jnp.dot(held.astype(BF16), both, preferred_element_type=F32)

    for i in range(rows):
        value = field[HALO + i]
        end[i] = value
        end_half[i] = value.astype(BF16)


def seed_kernel(end, obs, innovation, next_precision, next_start, seed, inner, outer, seed_half):
    rows = end.shape[0]
    for i in range(rows):
        held = end[i]
        following = next_precision[i].astype(F32) * (next_start[i].astype(F32) - held)
        misfit = obs[i].astype(F32) * (held - innovation[i].astype(F32))
        value = misfit - following
        seed[i] = value
        seed_half[i] = value.astype(BF16)
    take_sides(seed_half, inner, outer)


def adjoint_kernel(
    steps, seed, across, mate, diffuse, diffuse_mate, diffuse_across, mode_in, mode_out,
    carried,
    field, scaled, spread,
):
    rows, lon, lev = seed.shape
    whole = rows + 2 * HALO
    fill(field, spread, seed, diffuse, mate, across, diffuse_mate, diffuse_across)
    count = steps[0]
    for n in reversed(range(STEPS)):

        @pl.when(n < count)
        def _():
            edge = STEPS - 1 - n
            both = jnp.dot(mode_in[n], mode_out[n], preferred_element_type=F32).astype(BF16)
            for i in range(edge, whole - edge):
                held = field[i]
                coupled = held + lax.dot_general(
                    held.astype(BF16), both, (((1,), (1,)), ((), ())), preferred_element_type=F32
                )
                field[i] = coupled
                scaled[i] = spread[i].astype(F32) * coupled
            for i in range(edge + 1, whole - edge - 1):
                field[i] = field[i] + neighbours(scaled, i)

    for i in range(rows):
        carried[i] = field[HALO + i]


def gradient_kernel(carried, start, earlier, precision, pert, columns, gradient, partial):
    rows, lon, lev = carried.shape
    members = pert.shape[0]
    per = 128 // members
    blocks = partial.shape[0]
    selector = lane_selector(per)
    lane_group = iota((lon, 128), 1) // per
    total = jnp.zeros((blocks, 256), F32)
    for i in range(rows):
        jump = precision[i].astype(F32) * (start[i] - earlier[i].astype(F32))
        value = jump + carried[i]
        gradient[i] = value
        terms = jnp.zeros((lon, 128), F32)
        for k in range(members):
            term = jnp.sum(pert[k, i].astype(F32) * value, axis=1, keepdims=True)
            terms = jnp.where(lane_group == k, term, terms)
        column = columns[i : i + 1, :]
        block = one_hot_rows(column // per, blocks)
        rest_of = one_hot_rows(column % per, per)
        chosen = lax.dot_general(rest_of, selector, (((0,), (0,)), ((), ())), preferred_element_type=F32)
        pair = jnp.concatenate(split2(terms * chosen), axis=1)
        total = total + jnp.dot(block, pair, preferred_element_type=F32)
    partial[...] = total[:, :128] + total[:, 128:]


def swap(block, first):
    count = lax.axis_size("lat")
    route = []
    for i in range(first, count - 1, 2):
        route += [(i, i + 1), (i + 1, i)]
    return lax.ppermute(block, "lat", route)


def shifted(block, axis, distance):
    devices = range(lax.axis_size(axis))
    route = [(i - distance, i) for i in devices if i - distance in devices]
    return lax.ppermute(block, axis, route)


def body(
    incr_static,
    ens_pert,
    ens_weight,
    column_map,
    sub_steps,
    diffusion,
    mode_in,
    mode_out,
    model_precision,
    obs_precision,
    innovation,
):
    shape = incr_static.shape[1:]
    rows, lon, lev = shape
    members, _, per = ens_weight.shape
    windows = lax.axis_size("tm")
    half = jax.ShapeDtypeStruct(shape, BF16)
    edge = jax.ShapeDtypeStruct((HALO, lon, lev), BF16)
    full = jax.ShapeDtypeStruct(shape, F32)
    terms = jax.ShapeDtypeStruct((windows, members * per), F32)
    whole = (rows + 2 * HALO, lon, lev)
    dma = pltpu.SemaphoreType.DMA
    model_scratch = [
        pltpu.VMEM(whole, F32),
        pltpu.VMEM(whole, F32),
        pltpu.VMEM(whole, BF16),
    ]
    pert = ens_pert[:, 0]
    diffuse = diffusion[0]

    own, inner, outer = call(
        pack_kernel, (terms, edge, edge), [dma((2,))], [VM, HB], PACK_COST, COST
    )(ens_weight, diffuse)
    next_precision = shifted(model_precision[0], "tm", -1)
    diffuse_across = swap(outer, 1)
    diffuse_mate = swap(inner, 0)
    table = lax.all_to_all(own, "tm", 0, 0, tiled=True)
    start, start_half, inner, outer = call(
        start_kernel,
        (full, half, edge, edge),
        [],
        [VM] * 4,
        START_COST,
        COST,
    )(table, column_map, incr_static[0], pert)
    outer, inner, start_half, diffuse_across, diffuse_mate, next_precision = lax.optimization_barrier((outer, inner, start_half, diffuse_across, diffuse_mate, next_precision))
    across = swap(outer, 1)
    mate = swap(inner, 0)
    next_start = shifted(start_half, "tm", -1)
    end, end_half = call(
        forward_kernel, (full, half), model_scratch, [SM] + [VM] * 8, FORWARD_COST, COST
    )(sub_steps, start, across, mate, diffuse, diffuse_mate, diffuse_across, mode_in, mode_out)
    seed, inner, outer = call(
        seed_kernel,
        (full, edge, edge),
        [pltpu.VMEM(shape, BF16)],
        [VM] * 5,
        COST,
        COST,
    )(end, obs_precision[0], innovation[0], next_precision, next_start)
    across = swap(outer, 1)
    mate = swap(inner, 0)
    earlier = shifted(end_half, "tm", 1)
    carried = call(
        adjoint_kernel, full, model_scratch, [SM] + [VM] * 8, ADJOINT_COST, COST
    )(sub_steps, seed, across, mate, diffuse, diffuse_mate, diffuse_across, mode_in, mode_out)
    gradient, partial = call(
        gradient_kernel,
        (full, terms),
        [],
        [VM] * 6,
        COST,
        COST,
    )(carried, start, earlier, model_precision[0], pert, column_map)
    received = lax.all_to_all(partial, "tm", 0, 0, tiled=True)
    owned = jnp.sum(received, axis=0).reshape(members, 1, per)
    return (gradient[None], ens_weight + owned)


def solution(mesh):
    return jax.shard_map(
        body,
        mesh=mesh,
        in_specs=(
            P("tm", "lat", None, None),
            P(None, "tm", "lat", None, None),
            P(None, "lat", "tm"),
            P("lat", None),
            P("tm"),
            P("tm", "lat", None, None),
            P(),
            P(),
            P("tm", "lat", None, None),
            P("tm", "lat", None, None),
            P("tm", "lat", None, None),
        ),
        out_specs=(P("tm", "lat", None, None), P(None, "lat", "tm")),
        check_vma=False,
    )
```

```python
import functools

import jax
import jax.numpy as jnp
from jax import lax
from jax.experimental import pallas as pl
from jax.experimental.pallas import tpu as pltpu
from jax.sharding import PartitionSpec as P

STEPS = 4
HALO = STEPS
PAD = 16
F32 = jnp.float32
BF16 = jnp.bfloat16
VMEM_LIMIT = 40 * 1024 * 1024
COST = 1 << 20
PACK_COST = 1 << 33
START_COST = 1 << 20
FORWARD_COST = 1 << 34
SEED_COST = 1 << 33
ADJOINT_COST = 1 << 34

VM = pl.BlockSpec(memory_space=pltpu.VMEM)
SM = pl.BlockSpec(memory_space=pltpu.SMEM)
HB = pl.BlockSpec(memory_space=pltpu.HBM)


def iota(shape, dim):
    return lax.broadcasted_iota(jnp.int32, shape, dim)


def call(kernel, outs, scratch, specs, flops, nbytes):
    return pl.pallas_call(
        kernel,
        out_shape=outs,
        in_specs=specs,
        out_specs=jax.tree.map(lambda _: VM, outs),
        scratch_shapes=scratch,
        compiler_params=pltpu.CompilerParams(vmem_limit_bytes=VMEM_LIMIT),
        cost_estimate=pl.CostEstimate(flops=flops, bytes_accessed=nbytes, transcendentals=0),
    )


def split2(values):
    high = values.astype(BF16)
    low = (values - high.astype(F32)).astype(BF16)
    return high, low


def one_hot_rows(columns, count):
    return jnp.where(iota((count, columns.shape[1]), 0) == columns, 1.0, 0.0).astype(BF16)


def lane_selector(per):
    return jnp.where(iota((per, 128), 1) % per == iota((per, 128), 0), 1.0, 0.0).astype(BF16)


def group_spread(member, per):
    return jnp.where(iota((128, 128), 0) // per == member, 1.0, 0.0).astype(BF16)


def sides(rows):
    odd = lax.axis_index("lat") % 2
    return (1 - odd) * (rows - HALO), odd * (rows - HALO)


def pack_kernel(weight, diffuse, table, inner, outer, sems):
    rows = diffuse.shape[0]
    members, _, per = weight.shape
    near, far = sides(rows)
    copies = [
        pltpu.make_async_copy(diffuse.at[pl.ds(far, HALO)], outer, sems.at[0]),
        pltpu.make_async_copy(diffuse.at[pl.ds(near, HALO)], inner, sems.at[1]),
    ]
    for copy in copies:
        copy.start()
    held = weight[:, 0, :]
    selector = lane_selector(per)
    high = held.astype(BF16)
    rest = held - high.astype(F32)
    middle = rest.astype(BF16)
    low = (rest - middle.astype(F32)).astype(BF16)
    tiled = (
        jnp.dot(high, selector, preferred_element_type=F32)
        + jnp.dot(middle, selector, preferred_element_type=F32)
        + jnp.dot(low, selector, preferred_element_type=F32)
    )
    own = jnp.where(iota((members, 128), 1) // per == iota((members, 128), 0), tiled, 0.0)
    table[...] = jnp.broadcast_to(jnp.sum(own, axis=0, keepdims=True), table.shape)
    for copy in copies:
        copy.wait()


def take_sides(block, inner, outer):
    near, far = sides(block.shape[0])
    for i in range(HALO):
        inner[i] = block[near + i].astype(BF16)
        outer[i] = block[far + i].astype(BF16)


def start_kernel(table, columns, incr, pert, start, inner, outer, pair):
    rows, lon, lev = incr.shape
    members = pert.shape[0]
    blocks = table.shape[0]
    per = 128 // members
    high, low = split2(table[...])
    empty = jnp.zeros((blocks, 128), BF16)
    right = jnp.concatenate(
        [
            jnp.concatenate([high, low, empty], axis=1),
            jnp.concatenate([jnp.zeros((per, 256), BF16), lane_selector(per)], axis=1),
        ],
        axis=0,
    )
    for i in range(rows):
        column = columns[i : i + 1, :]
        left = jnp.concatenate([one_hot_rows(column // per, blocks), one_hot_rows(column % per, per)], axis=0)
        both = lax.dot_general(left, right, (((0,), (0,)), ((), ())), preferred_element_type=F32)
        mask = both[:, 256:]
        pair[i] = jnp.concatenate([both[:, :128] * mask, both[:, 128:256] * mask], axis=1).astype(BF16)
    for k in range(0, members, 2):
        spread = jnp.concatenate([group_spread(k, per), group_spread(k + 1, per)], axis=1)
        spread = jnp.concatenate([spread, spread], axis=0)
        for i in range(rows):
            weight = jnp.dot(pair[i], spread, preferred_element_type=F32)
            total = incr[i] if k == 0 else start[i]
            total = total + pert[k, i].astype(F32) * weight[:, :128]
            start[i] = total + pert[k + 1, i].astype(F32) * weight[:, 128:]
    take_sides(start, inner, outer)


def neighbours(field, i):
    middle = field[i]
    return (
        field[i - 1]
        + field[i + 1]
        + pltpu.roll(middle, 1, 0)
        + pltpu.roll(middle, middle.shape[0] - 1, 0)
        - 4.0 * middle
    )


def fill(field, spread, diffuse, mate, across, diffuse_mate, diffuse_across):
    rows = diffuse.shape[0]
    odd = lax.axis_index("lat") % 2
    mate_at = (1 - odd) * (HALO + rows)
    across_at = odd * (HALO + rows)
    for i in range(HALO):
        field[mate_at + i] = mate[i].astype(F32)
        spread[mate_at + i] = diffuse_mate[i]
        field[across_at + i] = across[i, : diffuse.shape[1]].astype(F32)
        spread[across_at + i] = diffuse_across[i]
    for i in range(rows):
        spread[HALO + i] = diffuse[i]


def forward_kernel(
    steps, start, across, mate, diffuse, diffuse_mate, diffuse_across, mode_in, mode_out,
    end, end_half,
    field, smooth, spread,
):
    rows, lon, lev = start.shape
    whole = rows + 2 * HALO
    fill(field, spread, diffuse, mate, across, diffuse_mate, diffuse_across)
    for i in range(rows):
        field[HALO + i] = start[i]
    count = steps[0]
    for n in range(STEPS):

        @pl.when(n < count)
        def _():
            both = jnp.dot(mode_in[n], mode_out[n], preferred_element_type=F32).astype(BF16)
            for i in range(n + 1, whole - n - 1):
                smooth[i] = field[i] + spread[i].astype(F32) * neighbours(field, i)
            for i in range(n + 1, whole - n - 1):
                held = smooth[i]
                field[i] = held + jnp.dot(held.astype(BF16), both, preferred_element_type=F32)

    for i in range(rows):
        value = field[HALO + i]
        end[i] = value
        end_half[i] = value.astype(BF16)


def seed_kernel(far_side, end, obs, innovation, next_precision, next_start, after, seed, seed_half):
    del after
    base = sides(end.shape[0])[far_side]
    for i in range(HALO):
        held = end[base + i]
        following = next_precision[base + i].astype(F32) * (next_start[i].astype(F32) - held)
        misfit = obs[base + i].astype(F32) * (held - innovation[base + i].astype(F32))
        value = misfit - following
        seed[i] = value
        seed_half[i, : value.shape[0]] = value.astype(BF16)
        if seed_half.shape[1] > value.shape[0]:
            seed_half[i, value.shape[0] :] = jnp.zeros((PAD, value.shape[1]), BF16)


def adjoint_kernel(
    steps, seed_inner, seed_outer, across, mate, diffuse, diffuse_mate, diffuse_across, mode_in, mode_out,
    carried,
    field, scaled, spread,
):
    rows, lon, lev = diffuse.shape
    whole = rows + 2 * HALO
    fill(field, spread, diffuse, mate, across, diffuse_mate, diffuse_across)
    near, far = sides(rows)
    for i in range(HALO):
        field[HALO + near + i] = seed_inner[i]
        field[HALO + far + i] = seed_outer[i]
    count = steps[0]
    for n in reversed(range(STEPS)):

        @pl.when(n < count)
        def _():
            edge = STEPS - 1 - n
            both = jnp.dot(mode_in[n], mode_out[n], preferred_element_type=F32).astype(BF16)
            for i in range(edge, whole - edge):
                held = field[i]
                coupled = held + lax.dot_general(
                    held.astype(BF16), both, (((1,), (1,)), ((), ())), preferred_element_type=F32
                )
                field[i] = coupled
                scaled[i] = spread[i].astype(F32) * coupled
            for i in range(edge + 1, whole - edge - 1):
                field[i] = field[i] + neighbours(scaled, i)

    for i in range(rows):
        carried[i] = field[HALO + i]


def gradient_kernel(carried, start, earlier, precision, pert, columns, gradient, partial):
    rows, lon, lev = carried.shape
    members = pert.shape[0]
    per = 128 // members
    blocks = partial.shape[0]
    selector = lane_selector(per)
    lane_group = iota((lon, 128), 1) // per
    total = jnp.zeros((blocks, 256), F32)
    for i in range(rows):
        jump = precision[i].astype(F32) * (start[i] - earlier[i].astype(F32))
        value = jump + carried[i]
        gradient[i] = value
        terms = jnp.zeros((lon, 128), F32)
        for k in range(members):
            term = jnp.sum(pert[k, i].astype(F32) * value, axis=1, keepdims=True)
            terms = jnp.where(lane_group == k, term, terms)
        column = columns[i : i + 1, :]
        block = one_hot_rows(column // per, blocks)
        rest_of = one_hot_rows(column % per, per)
        chosen = lax.dot_general(rest_of, selector, (((0,), (0,)), ((), ())), preferred_element_type=F32)
        pair = jnp.concatenate(split2(terms * chosen), axis=1)
        total = total + jnp.dot(block, pair, preferred_element_type=F32)
    partial[...] = total[:, :128] + total[:, 128:]


def swap(block, first):
    count = lax.axis_size("lat")
    route = []
    for i in range(first, count - 1, 2):
        route += [(i, i + 1), (i + 1, i)]
    return lax.ppermute(block, "lat", route)


def shifted(block, axis, distance):
    devices = range(lax.axis_size(axis))
    route = [(i - distance, i) for i in devices if i - distance in devices]
    return lax.ppermute(block, axis, route)


def body(
    incr_static,
    ens_pert,
    ens_weight,
    column_map,
    sub_steps,
    diffusion,
    mode_in,
    mode_out,
    model_precision,
    obs_precision,
    innovation,
):
    shape = incr_static.shape[1:]
    rows, lon, lev = shape
    members, _, per = ens_weight.shape
    windows = lax.axis_size("tm")
    half = jax.ShapeDtypeStruct(shape, BF16)
    edge = jax.ShapeDtypeStruct((HALO, lon, lev), BF16)
    edge_wide = jax.ShapeDtypeStruct((HALO, lon + PAD, lev), BF16)
    edge_full = jax.ShapeDtypeStruct((HALO, lon, lev), F32)
    full = jax.ShapeDtypeStruct(shape, F32)
    terms = jax.ShapeDtypeStruct((windows, members * per), F32)
    whole = (rows + 2 * HALO, lon, lev)
    dma = pltpu.SemaphoreType.DMA
    model_scratch = [
        pltpu.VMEM(whole, F32),
        pltpu.VMEM(whole, F32),
        pltpu.VMEM(whole, BF16),
    ]
    pert = ens_pert[:, 0]
    diffuse = diffusion[0]

    own, inner, outer = call(
        pack_kernel, (terms, edge, edge), [dma((2,))], [VM, HB], PACK_COST, COST
    )(ens_weight, diffuse)
    next_precision = shifted(model_precision[0], "tm", -1)
    diffuse_across = swap(outer, 1)
    diffuse_mate = swap(inner, 0)
    table = lax.all_to_all(own, "tm", 0, 0, tiled=True)
    start, inner, outer = call(
        start_kernel,
        (full, edge, edge),
        [pltpu.VMEM((rows, lon, 256), BF16)],
        [VM] * 4,
        START_COST,
        COST,
    )(table, column_map, incr_static[0], pert)
    outer, inner, diffuse_across, diffuse_mate, next_precision = lax.optimization_barrier((outer, inner, diffuse_across, diffuse_mate, next_precision))
    across = swap(outer, 1)
    mate = swap(inner, 0)
    next_outer = shifted(outer, "tm", -1)
    next_inner = shifted(inner, "tm", -1)
    end, end_half = call(
        forward_kernel, (full, half), model_scratch, [SM] + [VM] * 8, FORWARD_COST, COST
    )(sub_steps, start, across, mate, diffuse, diffuse_mate, diffuse_across, mode_in, mode_out)
    seed_outer, outer = call(
        functools.partial(seed_kernel, 1), (edge_full, edge_wide), [], [VM] * 5 + [HB], COST, COST
    )(end, obs_precision[0], innovation[0], next_precision, next_outer, end)
    seed_inner, inner = call(
        functools.partial(seed_kernel, 0), (edge_full, edge), [], [VM] * 5 + [HB], SEED_COST, COST
    )(end, obs_precision[0], innovation[0], next_precision, next_inner, seed_outer)
    across = swap(outer, 1)
    mate = swap(inner, 0)
    earlier = shifted(end_half, "tm", 1)
    carried = call(
        adjoint_kernel, full, model_scratch, [SM] + [VM] * 9, ADJOINT_COST, COST
    )(
        sub_steps, seed_inner, seed_outer, across, mate, diffuse, diffuse_mate, diffuse_across,
        mode_in, mode_out,
    )
    gradient, partial = call(
        gradient_kernel,
        (full, terms),
        [],
        [VM] * 6,
        COST,
        COST,
    )(carried, start, earlier, model_precision[0], pert, column_map)
    received = lax.all_to_all(partial, "tm", 0, 0, tiled=True)
    owned = jnp.sum(received, axis=0).reshape(members, 1, per)
    return (gradient[None], ens_weight + owned)


def solution(mesh):
    return jax.shard_map(
        body,
        mesh=mesh,
        in_specs=(
            P("tm", "lat", None, None),
            P(None, "tm", "lat", None, None),
            P(None, "lat", "tm"),
            P("lat", None),
            P("tm"),
            P("tm", "lat", None, None),
            P(),
            P(),
            P("tm", "lat", None, None),
            P("tm", "lat", None, None),
            P("tm", "lat", None, None),
        ),
        out_specs=(P("tm", "lat", None, None), P(None, "lat", "tm")),
        check_vma=False,
    )
```

```python
import functools

import jax
import jax.numpy as jnp
from jax import lax
from jax.experimental import pallas as pl
from jax.experimental.pallas import tpu as pltpu
from jax.sharding import PartitionSpec as P

STEPS = 4
HALO = STEPS
PAD = 16
F32 = jnp.float32
BF16 = jnp.bfloat16
VMEM_LIMIT = 40 * 1024 * 1024
COST = 1 << 20
PACK_COST = 1 << 33
START_COST = 1 << 20
FORWARD_COST = 1 << 34
SEED_COST = 1 << 33
ADJOINT_COST = 1 << 20

VM = pl.BlockSpec(memory_space=pltpu.VMEM)
SM = pl.BlockSpec(memory_space=pltpu.SMEM)
HB = pl.BlockSpec(memory_space=pltpu.HBM)


def iota(shape, dim):
    return lax.broadcasted_iota(jnp.int32, shape, dim)


def call(kernel, outs, scratch, specs, flops, nbytes, out_specs=None, aliases={}):
    return pl.pallas_call(
        kernel,
        out_shape=outs,
        in_specs=specs,
        out_specs=out_specs or jax.tree.map(lambda _: VM, outs),
        input_output_aliases=aliases,
        scratch_shapes=scratch,
        compiler_params=pltpu.CompilerParams(vmem_limit_bytes=VMEM_LIMIT),
        cost_estimate=pl.CostEstimate(flops=flops, bytes_accessed=nbytes, transcendentals=0),
    )


def split2(values):
    high = values.astype(BF16)
    low = (values - high.astype(F32)).astype(BF16)
    return high, low


def one_hot_rows(columns, count):
    return jnp.where(iota((count, columns.shape[1]), 0) == columns, 1.0, 0.0).astype(BF16)


def lane_selector(per):
    return jnp.where(iota((per, 128), 1) % per == iota((per, 128), 0), 1.0, 0.0).astype(BF16)


def group_spread(member, per):
    return jnp.where(iota((128, 128), 0) // per == member, 1.0, 0.0).astype(BF16)


def sides(rows):
    odd = lax.axis_index("lat") % 2
    return (1 - odd) * (rows - HALO), odd * (rows - HALO)


def pack_kernel(weight, diffuse, table, inner, outer, sems):
    rows = diffuse.shape[0]
    members, _, per = weight.shape
    near, far = sides(rows)
    copies = [
        pltpu.make_async_copy(diffuse.at[pl.ds(far, HALO)], outer, sems.at[0]),
        pltpu.make_async_copy(diffuse.at[pl.ds(near, HALO)], inner, sems.at[1]),
    ]
    for copy in copies:
        copy.start()
    held = weight[:, 0, :]
    selector = lane_selector(per)
    high = held.astype(BF16)
    rest = held - high.astype(F32)
    middle = rest.astype(BF16)
    low = (rest - middle.astype(F32)).astype(BF16)
    tiled = (
        jnp.dot(high, selector, preferred_element_type=F32)
        + jnp.dot(middle, selector, preferred_element_type=F32)
        + jnp.dot(low, selector, preferred_element_type=F32)
    )
    own = jnp.where(iota((members, 128), 1) // per == iota((members, 128), 0), tiled, 0.0)
    table[...] = jnp.broadcast_to(jnp.sum(own, axis=0, keepdims=True), table.shape)
    for copy in copies:
        copy.wait()


def take_sides(block, inner, outer):
    near, far = sides(block.shape[0])
    for i in range(HALO):
        inner[i] = block[near + i].astype(BF16)
        outer[i] = block[far + i].astype(BF16)


def start_kernel(table, columns, incr, pert, start, inner, outer, masks, pair):
    rows, lon, lev = incr.shape
    members = pert.shape[0]
    blocks = table.shape[0]
    per = 128 // members
    high, low = split2(table[...])
    empty = jnp.zeros((blocks, 128), BF16)
    right = jnp.concatenate(
        [
            jnp.concatenate([high, low, empty], axis=1),
            jnp.concatenate([jnp.zeros((per, 256), BF16), lane_selector(per)], axis=1),
        ],
        axis=0,
    )
    for i in range(rows):
        column = columns[i : i + 1, :]
        left = jnp.concatenate([one_hot_rows(column // per, blocks), one_hot_rows(column % per, per)], axis=0)
        both = lax.dot_general(left, right, (((0,), (0,)), ((), ())), preferred_element_type=F32)
        mask = both[:, 256:]
        masks[i] = mask.astype(BF16)
        pair[i] = jnp.concatenate([both[:, :128] * mask, both[:, 128:256] * mask], axis=1).astype(BF16)
    for k in range(0, members, 2):
        spread = jnp.concatenate([group_spread(k, per), group_spread(k + 1, per)], axis=1)
        spread = jnp.concatenate([spread, spread], axis=0)
        for i in range(rows):
            weight = jnp.dot(pair[i], spread, preferred_element_type=F32)
            total = incr[i] if k == 0 else start[i]
            total = total + pert[k, i].astype(F32) * weight[:, :128]
            start[i] = total + pert[k + 1, i].astype(F32) * weight[:, 128:]
    take_sides(start, inner, outer)


def neighbours(field, i):
    middle = field[i]
    return (
        field[i - 1]
        + field[i + 1]
        + pltpu.roll(middle, 1, 0)
        + pltpu.roll(middle, middle.shape[0] - 1, 0)
        - 4.0 * middle
    )


def fill(field, spread, diffuse, mate, across, diffuse_mate, diffuse_across):
    rows = diffuse.shape[0]
    odd = lax.axis_index("lat") % 2
    mate_at = (1 - odd) * (HALO + rows)
    across_at = odd * (HALO + rows)
    for i in range(HALO):
        field[mate_at + i] = mate[i].astype(F32)
        spread[mate_at + i] = diffuse_mate[i]
        field[across_at + i] = across[i, : diffuse.shape[1]].astype(F32)
        spread[across_at + i] = diffuse_across[i]
    for i in range(rows):
        spread[HALO + i] = diffuse[i]


def forward_kernel(
    steps, start, across, mate, diffuse, diffuse_mate, diffuse_across, mode_in, mode_out,
    end, end_inner, end_outer,
    field, smooth, spread,
):
    rows, lon, lev = start.shape
    whole = rows + 2 * HALO
    fill(field, spread, diffuse, mate, across, diffuse_mate, diffuse_across)
    for i in range(rows):
        field[HALO + i] = start[i]
    count = steps[0]
    for n in range(STEPS):

        @pl.when(n < count)
        def _():
            both = jnp.dot(mode_in[n], mode_out[n], preferred_element_type=F32).astype(BF16)
            for i in range(n + 1, whole - n - 1):
                smooth[i] = field[i] + spread[i].astype(F32) * neighbours(field, i)
            for i in range(n + 1, whole - n - 1):
                held = smooth[i]
                field[i] = held + jnp.dot(held.astype(BF16), both, preferred_element_type=F32)

    for i in range(rows):
        value = field[HALO + i]
        end[i] = value
    take_sides(end, end_inner, end_outer)


def seed_kernel(far_side, end, obs, innovation, next_precision, next_start, after, seed, seed_half):
    del after
    base = sides(end.shape[0])[far_side]
    for i in range(HALO):
        held = end[base + i]
        following = next_precision[base + i].astype(F32) * (next_start[i].astype(F32) - held)
        misfit = obs[base + i].astype(F32) * (held - innovation[base + i].astype(F32))
        value = misfit - following
        seed[i] = value
        seed_half[i, : value.shape[0]] = value.astype(BF16)
        if seed_half.shape[1] > value.shape[0]:
            seed_half[i, value.shape[0] :] = jnp.zeros((PAD, value.shape[1]), BF16)


def adjoint_kernel(
    steps, seed_inner, seed_outer, across, mate, diffuse, diffuse_mate, diffuse_across, mode_in, mode_out,
    carried,
    field, scaled, spread,
):
    rows, lon, lev = diffuse.shape
    whole = rows + 2 * HALO
    fill(field, spread, diffuse, mate, across, diffuse_mate, diffuse_across)
    near, far = sides(rows)
    for i in range(HALO):
        field[HALO + near + i] = seed_inner[i]
        field[HALO + far + i] = seed_outer[i]
    count = steps[0]
    for n in reversed(range(STEPS)):

        @pl.when(n < count)
        def _():
            edge = STEPS - 1 - n
            both = jnp.dot(mode_in[n], mode_out[n], preferred_element_type=F32).astype(BF16)
            for i in range(edge, whole - edge):
                held = field[i]
                coupled = held + lax.dot_general(
                    held.astype(BF16), both, (((1,), (1,)), ((), ())), preferred_element_type=F32
                )
                field[i] = coupled
                scaled[i] = spread[i].astype(F32) * coupled
            for i in range(edge + 1, whole - edge - 1):
                field[i] = field[i] + neighbours(scaled, i)

    for i in range(rows):
        carried[i] = field[HALO + i]


def gradient_kernel(far_side, carried, start, earlier, precision, pert, columns, mask, *rest):
    gradient, partial, stage, sems = rest[-4:]
    rows, lon, lev = carried.shape
    members = pert.shape[0]
    per = 128 // members
    blocks = partial.shape[0]
    base = sides(rows)[far_side]
    copies = []
    for i in range(HALO):
        row = base + i
        jump = precision[row].astype(F32) * (start[row] - earlier[i].astype(F32))
        stage[i] = jump + carried[row]
        copies.append(pltpu.make_async_copy(stage.at[i], gradient.at[row], sems.at[i]))
        copies[i].start()
    lane_group = iota((lon, 128), 1) // per
    total = jnp.zeros((blocks, 256), F32)
    for i in range(HALO):
        row = base + i
        value = stage[i]
        terms = jnp.zeros((lon, 128), F32)
        for k in range(members):
            term = jnp.sum(pert[k, row].astype(F32) * value, axis=1, keepdims=True)
            terms = jnp.where(lane_group == k, term, terms)
        block = one_hot_rows(columns[pl.ds(row, 1), :] // per, blocks)
        pair = jnp.concatenate(split2(terms * mask[row].astype(F32)), axis=1)
        total = total + jnp.dot(block, pair, preferred_element_type=F32)
    summed = total[:, :128] + total[:, 128:]
    partial[...] = summed if far_side else rest[0][...] + summed
    for copy in copies:
        copy.wait()


def swap(block, first):
    count = lax.axis_size("lat")
    route = []
    for i in range(first, count - 1, 2):
        route += [(i, i + 1), (i + 1, i)]
    return lax.ppermute(block, "lat", route)


def shifted(block, axis, distance):
    devices = range(lax.axis_size(axis))
    route = [(i - distance, i) for i in devices if i - distance in devices]
    return lax.ppermute(block, axis, route)


def body(
    incr_static,
    ens_pert,
    ens_weight,
    column_map,
    sub_steps,
    diffusion,
    mode_in,
    mode_out,
    model_precision,
    obs_precision,
    innovation,
):
    shape = incr_static.shape[1:]
    rows, lon, lev = shape
    members, _, per = ens_weight.shape
    windows = lax.axis_size("tm")
    half = jax.ShapeDtypeStruct(shape, BF16)
    edge = jax.ShapeDtypeStruct((HALO, lon, lev), BF16)
    edge_wide = jax.ShapeDtypeStruct((HALO, lon + PAD, lev), BF16)
    edge_full = jax.ShapeDtypeStruct((HALO, lon, lev), F32)
    full = jax.ShapeDtypeStruct(shape, F32)
    terms = jax.ShapeDtypeStruct((windows, members * per), F32)
    whole = (rows + 2 * HALO, lon, lev)
    dma = pltpu.SemaphoreType.DMA
    model_scratch = [
        pltpu.VMEM(whole, F32),
        pltpu.VMEM(whole, F32),
        pltpu.VMEM(whole, BF16),
    ]
    pert = ens_pert[:, 0]
    diffuse = diffusion[0]

    own, inner, outer = call(
        pack_kernel, (terms, edge, edge), [dma((2,))], [VM, HB], PACK_COST, COST
    )(ens_weight, diffuse)
    next_precision = shifted(model_precision[0], "tm", -1)
    diffuse_across = swap(outer, 1)
    diffuse_mate = swap(inner, 0)
    table = lax.all_to_all(own, "tm", 0, 0, tiled=True)
    start, inner, outer, mask = call(
        start_kernel,
        (full, edge, edge, half),
        [pltpu.VMEM((rows, lon, 256), BF16)],
        [VM] * 4,
        START_COST,
        COST,
    )(table, column_map, incr_static[0], pert)
    outer, inner, diffuse_across, diffuse_mate, next_precision = lax.optimization_barrier((outer, inner, diffuse_across, diffuse_mate, next_precision))
    across = swap(outer, 1)
    mate = swap(inner, 0)
    next_outer = shifted(outer, "tm", -1)
    next_inner = shifted(inner, "tm", -1)
    end, end_inner, end_outer = call(
        forward_kernel, (full, edge, edge), model_scratch, [SM] + [VM] * 8, FORWARD_COST, COST
    )(sub_steps, start, across, mate, diffuse, diffuse_mate, diffuse_across, mode_in, mode_out)
    seed_outer, outer = call(
        functools.partial(seed_kernel, 1), (edge_full, edge_wide), [], [VM] * 5 + [HB], COST, COST
    )(end, obs_precision[0], innovation[0], next_precision, next_outer, end)
    seed_inner, inner = call(
        functools.partial(seed_kernel, 0), (edge_full, edge), [], [VM] * 5 + [HB], SEED_COST, COST
    )(end, obs_precision[0], innovation[0], next_precision, next_inner, seed_outer)
    across = swap(outer, 1)
    mate = swap(inner, 0)
    earlier_outer = shifted(end_outer, "tm", 1)
    end_inner, inner = lax.optimization_barrier((end_inner, inner))
    earlier_inner = shifted(end_inner, "tm", 1)
    carried = call(
        adjoint_kernel, full, model_scratch, [SM] + [VM] * 9, ADJOINT_COST, COST
    )(
        sub_steps, seed_inner, seed_outer, across, mate, diffuse, diffuse_mate, diffuse_across,
        mode_in, mode_out,
    )
    outs = (full, terms)
    scratch = [pltpu.VMEM(edge_full.shape, F32), dma((HALO,))]
    gradient, partial = call(
        functools.partial(gradient_kernel, 1), outs, scratch, [VM] * 7, COST, COST, (HB, VM)
    )(carried, start, earlier_outer, model_precision[0], pert, column_map, mask)
    gradient, partial = call(
        functools.partial(gradient_kernel, 0), outs, scratch, [VM] * 8 + [HB], COST, COST, (HB, VM), {8: 0}
    )(carried, start, earlier_inner, model_precision[0], pert, column_map, mask, partial, gradient)
    received = lax.all_to_all(partial, "tm", 0, 0, tiled=True)
    owned = jnp.sum(received, axis=0).reshape(members, 1, per)
    return (gradient[None], ens_weight + owned)


def solution(mesh):
    return jax.shard_map(
        body,
        mesh=mesh,
        in_specs=(
            P("tm", "lat", None, None),
            P(None, "tm", "lat", None, None),
            P(None, "lat", "tm"),
            P("lat", None),
            P("tm"),
            P("tm", "lat", None, None),
            P(),
            P(),
            P("tm", "lat", None, None),
            P("tm", "lat", None, None),
            P("tm", "lat", None, None),
        ),
        out_specs=(P("tm", "lat", None, None), P(None, "lat", "tm")),
        check_vma=False,
    )
```

```python
import functools

import jax
import jax.numpy as jnp
from jax import lax
from jax.experimental import pallas as pl
from jax.experimental.pallas import tpu as pltpu
from jax.sharding import PartitionSpec as P

STEPS = 4
HALO = STEPS
PAD = 16
F32 = jnp.float32
BF16 = jnp.bfloat16
VMEM_LIMIT = 40 * 1024 * 1024
COST = 1 << 20
PACK_COST = 1 << 33
START_COST = 1 << 20
FORWARD_COST = 1 << 34
SEED_COST = 1 << 33
ADJOINT_COST = 1 << 20

VM = pl.BlockSpec(memory_space=pltpu.VMEM)
SM = pl.BlockSpec(memory_space=pltpu.SMEM)
HB = pl.BlockSpec(memory_space=pltpu.HBM)


def iota(shape, dim):
    return lax.broadcasted_iota(jnp.int32, shape, dim)


def call(kernel, outs, scratch, specs, flops, nbytes, out_specs=None, aliases={}):
    return pl.pallas_call(
        kernel,
        out_shape=outs,
        in_specs=specs,
        out_specs=out_specs or jax.tree.map(lambda _: VM, outs),
        input_output_aliases=aliases,
        scratch_shapes=scratch,
        compiler_params=pltpu.CompilerParams(vmem_limit_bytes=VMEM_LIMIT),
        cost_estimate=pl.CostEstimate(flops=flops, bytes_accessed=nbytes, transcendentals=0),
    )


def split2(values):
    high = values.astype(BF16)
    low = (values - high.astype(F32)).astype(BF16)
    return high, low


def one_hot_rows(columns, count):
    return jnp.where(iota((count, columns.shape[1]), 0) == columns, 1.0, 0.0).astype(BF16)


def lane_selector(per):
    return jnp.where(iota((per, 128), 1) % per == iota((per, 128), 0), 1.0, 0.0).astype(BF16)


def group_spread(member, per):
    return jnp.where(iota((128, 128), 0) // per == member, 1.0, 0.0).astype(BF16)


def sides(rows):
    odd = lax.axis_index("lat") % 2
    return (1 - odd) * (rows - HALO), odd * (rows - HALO)


def pack_kernel(weight, diffuse, table, inner, outer, sems):
    rows = diffuse.shape[0]
    members, _, per = weight.shape
    near, far = sides(rows)
    copies = [
        pltpu.make_async_copy(diffuse.at[pl.ds(far, HALO)], outer, sems.at[0]),
        pltpu.make_async_copy(diffuse.at[pl.ds(near, HALO)], inner, sems.at[1]),
    ]
    for copy in copies:
        copy.start()
    held = weight[:, 0, :]
    selector = lane_selector(per)
    high = held.astype(BF16)
    rest = held - high.astype(F32)
    middle = rest.astype(BF16)
    low = (rest - middle.astype(F32)).astype(BF16)
    tiled = (
        jnp.dot(high, selector, preferred_element_type=F32)
        + jnp.dot(middle, selector, preferred_element_type=F32)
        + jnp.dot(low, selector, preferred_element_type=F32)
    )
    own = jnp.where(iota((members, 128), 1) // per == iota((members, 128), 0), tiled, 0.0)
    table[...] = jnp.broadcast_to(jnp.sum(own, axis=0, keepdims=True), table.shape)
    for copy in copies:
        copy.wait()


def take_sides(block, inner, outer):
    near, far = sides(block.shape[0])
    for i in range(HALO):
        inner[i] = block[near + i].astype(BF16)
        outer[i] = block[far + i].astype(BF16)


def start_kernel(table, columns, incr, pert, start, inner, outer, masks, pair):
    rows, lon, lev = incr.shape
    members = pert.shape[0]
    blocks = table.shape[0]
    per = 128 // members
    high, low = split2(table[...])
    empty = jnp.zeros((blocks, 128), BF16)
    right = jnp.concatenate(
        [
            jnp.concatenate([high, low, empty], axis=1),
            jnp.concatenate([jnp.zeros((per, 256), BF16), lane_selector(per)], axis=1),
        ],
        axis=0,
    )
    for i in range(rows):
        column = columns[i : i + 1, :]
        left = jnp.concatenate([one_hot_rows(column // per, blocks), one_hot_rows(column % per, per)], axis=0)
        both = lax.dot_general(left, right, (((0,), (0,)), ((), ())), preferred_element_type=F32)
        mask = both[:, 256:]
        masks[i] = mask.astype(BF16)
        pair[i] = jnp.concatenate([both[:, :128] * mask, both[:, 128:256] * mask], axis=1).astype(BF16)
    for k in range(0, members, 2):
        spread = jnp.concatenate([group_spread(k, per), group_spread(k + 1, per)], axis=1)
        spread = jnp.concatenate([spread, spread], axis=0)
        for i in range(rows):
            weight = jnp.dot(pair[i], spread, preferred_element_type=F32)
            total = incr[i] if k == 0 else start[i]
            total = total + pert[k, i].astype(F32) * weight[:, :128]
            start[i] = total + pert[k + 1, i].astype(F32) * weight[:, 128:]
    take_sides(start, inner, outer)


def neighbours(row, i):
    middle = row(i)
    return (
        row(i - 1)
        + row(i + 1)
        + pltpu.roll(middle, 1, 0)
        + pltpu.roll(middle, middle.shape[0] - 1, 0)
        - 4.0 * middle
    )


def joined(own, around):
    rows = own.shape[0]
    return lambda i: own[i - HALO] if HALO <= i < HALO + rows else around[i]


def fill(field, spread, diffuse, mate, across, diffuse_mate, diffuse_across):
    rows = diffuse.shape[0]
    odd = lax.axis_index("lat") % 2
    mate_at = (1 - odd) * (HALO + rows)
    across_at = odd * (HALO + rows)
    for i in range(HALO):
        field[mate_at + i] = mate[i].astype(F32)
        spread[mate_at + i] = diffuse_mate[i]
        field[across_at + i] = across[i, : diffuse.shape[1]].astype(F32)
        spread[across_at + i] = diffuse_across[i]


def forward_kernel(
    steps, start, across, mate, diffuse, diffuse_mate, diffuse_across, mode_in, mode_out,
    end, end_inner, end_outer,
    field, smooth, spread,
):
    rows, lon, lev = start.shape
    whole = rows + 2 * HALO
    fill(field, spread, diffuse, mate, across, diffuse_mate, diffuse_across)
    coefficient = joined(diffuse, spread)
    count = steps[0]
    for n in range(STEPS):

        @pl.when(jnp.logical_or(n == 0, n < count))
        def _():
            both = jnp.dot(mode_in[n], mode_out[n], preferred_element_type=F32).astype(BF16)
            row = joined(start, field) if n == 0 else field.__getitem__
            for i in range(n + 1, whole - n - 1):
                smooth[i] = row(i) + coefficient(i).astype(F32) * neighbours(row, i)
            for i in range(n + 1, whole - n - 1):
                held = smooth[i]
                field[i] = held + jnp.dot(held.astype(BF16), both, preferred_element_type=F32)

    for i in range(rows):
        value = field[HALO + i]
        end[i] = value
    take_sides(end, end_inner, end_outer)


def seed_kernel(far_side, end, obs, innovation, next_precision, next_start, after, seed, seed_half):
    del after
    base = sides(end.shape[0])[far_side]
    for i in range(HALO):
        held = end[base + i]
        following = next_precision[base + i].astype(F32) * (next_start[i].astype(F32) - held)
        misfit = obs[base + i].astype(F32) * (held - innovation[base + i].astype(F32))
        value = misfit - following
        seed[i] = value
        seed_half[i, : value.shape[0]] = value.astype(BF16)
        if seed_half.shape[1] > value.shape[0]:
            seed_half[i, value.shape[0] :] = jnp.zeros((PAD, value.shape[1]), BF16)


def adjoint_kernel(
    steps, seed_inner, seed_outer, across, mate, diffuse, diffuse_mate, diffuse_across, mode_in, mode_out,
    carried,
    field, scaled, spread,
):
    rows, lon, lev = diffuse.shape
    whole = rows + 2 * HALO
    fill(field, spread, diffuse, mate, across, diffuse_mate, diffuse_across)
    near, far = sides(rows)
    for i in range(HALO):
        field[HALO + near + i] = seed_inner[i]
        field[HALO + far + i] = seed_outer[i]
    coefficient = joined(diffuse, spread)
    count = steps[0]
    for n in reversed(range(STEPS)):

        @pl.when(jnp.logical_or(n == 0, n < count))
        def _():
            edge = STEPS - 1 - n
            both = jnp.dot(mode_in[n], mode_out[n], preferred_element_type=F32).astype(BF16)
            for i in range(edge, whole - edge):
                held = field[i]
                coupled = held + lax.dot_general(
                    held.astype(BF16), both, (((1,), (1,)), ((), ())), preferred_element_type=F32
                )
                if edge < i < whole - edge - 1:
                    field[i] = coupled
                scaled[i] = coefficient(i).astype(F32) * coupled
            for i in range(edge + 1, whole - edge - 1):
                value = field[i] + neighbours(scaled.__getitem__, i)
                if n == 0:
                    carried[i - HALO] = value
                else:
                    field[i] = value


def gradient_kernel(far_side, carried, start, earlier, precision, pert, columns, mask, *rest):
    gradient, partial, stage, sems = rest[-4:]
    rows, lon, lev = carried.shape
    members = pert.shape[0]
    per = 128 // members
    blocks = partial.shape[0]
    base = sides(rows)[far_side]
    copies = []
    for i in range(HALO):
        row = base + i
        jump = precision[row].astype(F32) * (start[row] - earlier[i].astype(F32))
        stage[i] = jump + carried[row]
        copies.append(pltpu.make_async_copy(stage.at[i], gradient.at[row], sems.at[i]))
        copies[i].start()
    lane_group = iota((lon, 128), 1) // per
    total = jnp.zeros((blocks, 256), F32)
    for i in range(HALO):
        row = base + i
        value = stage[i]
        terms = jnp.zeros((lon, 128), F32)
        for k in range(members):
            term = jnp.sum(pert[k, row].astype(F32) * value, axis=1, keepdims=True)
            terms = jnp.where(lane_group == k, term, terms)
        block = one_hot_rows(columns[pl.ds(row, 1), :] // per, blocks)
        pair = jnp.concatenate(split2(terms * mask[row].astype(F32)), axis=1)
        total = total + jnp.dot(block, pair, preferred_element_type=F32)
    summed = total[:, :128] + total[:, 128:]
    partial[...] = summed if far_side else rest[0][...] + summed
    for copy in copies:
        copy.wait()


def swap(block, first):
    count = lax.axis_size("lat")
    route = []
    for i in range(first, count - 1, 2):
        route += [(i, i + 1), (i + 1, i)]
    return lax.ppermute(block, "lat", route)


def shifted(block, axis, distance):
    devices = range(lax.axis_size(axis))
    route = [(i - distance, i) for i in devices if i - distance in devices]
    return lax.ppermute(block, axis, route)


def body(
    incr_static,
    ens_pert,
    ens_weight,
    column_map,
    sub_steps,
    diffusion,
    mode_in,
    mode_out,
    model_precision,
    obs_precision,
    innovation,
):
    shape = incr_static.shape[1:]
    rows, lon, lev = shape
    members, _, per = ens_weight.shape
    windows = lax.axis_size("tm")
    half = jax.ShapeDtypeStruct(shape, BF16)
    edge = jax.ShapeDtypeStruct((HALO, lon, lev), BF16)
    edge_wide = jax.ShapeDtypeStruct((HALO, lon + PAD, lev), BF16)
    edge_full = jax.ShapeDtypeStruct((HALO, lon, lev), F32)
    full = jax.ShapeDtypeStruct(shape, F32)
    terms = jax.ShapeDtypeStruct((windows, members * per), F32)
    whole = (rows + 2 * HALO, lon, lev)
    dma = pltpu.SemaphoreType.DMA
    model_scratch = [
        pltpu.VMEM(whole, F32),
        pltpu.VMEM(whole, F32),
        pltpu.VMEM(whole, BF16),
    ]
    pert = ens_pert[:, 0]
    diffuse = diffusion[0]

    own, inner, outer = call(
        pack_kernel, (terms, edge, edge), [dma((2,))], [VM, HB], PACK_COST, COST
    )(ens_weight, diffuse)
    next_precision = shifted(model_precision[0], "tm", -1)
    diffuse_across = swap(outer, 1)
    diffuse_mate = swap(inner, 0)
    table = lax.all_to_all(own, "tm", 0, 0, tiled=True)
    start, inner, outer, mask = call(
        start_kernel,
        (full, edge, edge, half),
        [pltpu.VMEM((rows, lon, 256), BF16)],
        [VM] * 4,
        START_COST,
        COST,
    )(table, column_map, incr_static[0], pert)
    outer, inner, diffuse_across, diffuse_mate, next_precision = lax.optimization_barrier((outer, inner, diffuse_across, diffuse_mate, next_precision))
    across = swap(outer, 1)
    mate = swap(inner, 0)
    next_outer = shifted(outer, "tm", -1)
    next_inner = shifted(inner, "tm", -1)
    end, end_inner, end_outer = call(
        forward_kernel, (full, edge, edge), model_scratch, [SM] + [VM] * 8, FORWARD_COST, COST
    )(sub_steps, start, across, mate, diffuse, diffuse_mate, diffuse_across, mode_in, mode_out)
    seed_outer, outer = call(
        functools.partial(seed_kernel, 1), (edge_full, edge_wide), [], [VM] * 5 + [HB], COST, COST
    )(end, obs_precision[0], innovation[0], next_precision, next_outer, end)
    seed_inner, inner = call(
        functools.partial(seed_kernel, 0), (edge_full, edge), [], [VM] * 5 + [HB], SEED_COST, COST
    )(end, obs_precision[0], innovation[0], next_precision, next_inner, seed_outer)
    across = swap(outer, 1)
    mate = swap(inner, 0)
    earlier_outer = shifted(end_outer, "tm", 1)
    end_inner, inner = lax.optimization_barrier((end_inner, inner))
    earlier_inner = shifted(end_inner, "tm", 1)
    carried = call(
        adjoint_kernel, full, model_scratch, [SM] + [VM] * 9, ADJOINT_COST, COST
    )(
        sub_steps, seed_inner, seed_outer, across, mate, diffuse, diffuse_mate, diffuse_across,
        mode_in, mode_out,
    )
    outs = (full, terms)
    scratch = [pltpu.VMEM(edge_full.shape, F32), dma((HALO,))]
    gradient, partial = call(
        functools.partial(gradient_kernel, 1), outs, scratch, [VM] * 7, COST, COST, (HB, VM)
    )(carried, start, earlier_outer, model_precision[0], pert, column_map, mask)
    gradient, partial = call(
        functools.partial(gradient_kernel, 0), outs, scratch, [VM] * 8 + [HB], COST, COST, (HB, VM), {8: 0}
    )(carried, start, earlier_inner, model_precision[0], pert, column_map, mask, partial, gradient)
    received = lax.all_to_all(partial, "tm", 0, 0, tiled=True)
    owned = jnp.sum(received, axis=0).reshape(members, 1, per)
    return (gradient[None], ens_weight + owned)


def solution(mesh):
    return jax.shard_map(
        body,
        mesh=mesh,
        in_specs=(
            P("tm", "lat", None, None),
            P(None, "tm", "lat", None, None),
            P(None, "lat", "tm"),
            P("lat", None),
            P("tm"),
            P("tm", "lat", None, None),
            P(),
            P(),
            P("tm", "lat", None, None),
            P("tm", "lat", None, None),
            P("tm", "lat", None, None),
        ),
        out_specs=(P("tm", "lat", None, None), P(None, "lat", "tm")),
        check_vma=False,
    )
```
